32 devices in a mesh: seq: 4 (over y, core), wide: 8 (over z, x).
Axes of the slice: x: 2, y: 2, z: 4, core: 2. Of those that a mesh axis runs over, the one named last changes fastest.
Arguments:
- qkv_proj: bfloat16 [3, 2, 2048, 4096], P(None, None, ('seq', 'wide')), may hold values from -6 to 6
- conv_kernel: float32 [3, 4, 4096], replicated, may hold values from -3 to 3
- qk_gain: float32 [2, 8, 512], P(None, 'wide'), may hold values from 0.4 to 2.5
- fast_init: float32 [3, 8, 512, 512], P(None, 'wide'), may hold values from -0.25 to 0.25
- step_size: float32 [8], P('wide'), may hold values from 0.2 to 1
Outputs:
- fast_out: bfloat16 [2, 2048, 4096], P(None, 'seq', 'wide')
The draws below stay inside these ranges and needn't reach their ends.
All inputs are finite; a program needn't handle non-finite values.
Results may differ from the reference program's by a relative error of at most 0.004.
Values may be sent and summed in bfloat16 or wider, within the bound.
A program may use at most 128 MiB of HBM per device.

```python
import math
import jax
import jax.numpy as jnp
from jax import lax

HEAD = 512
HEADS = 8
D = 4096
GROUPS = 2
KW = 4
GROUP = 2048


def block_levels(rng, dims, split, low, top_value):
    def one(axis_at, parts):
        heights = jax.random.uniform(jax.random.fold_in(jax.random.fold_in(rng, 6), axis_at), (parts,), jnp.float32, low / len(split), top_value / len(split))
        return jnp.repeat(jnp.exp(heights), dims[axis_at] // parts).reshape((-1,) + (1,) * (len(dims) - axis_at - 1))

    gain = one(*split[0])
    for cut in split[1:]:
        gain = gain * one(*cut)
    return gain


def scatter_about(stream_key, dims, spread, limit, shards=(), kind=jnp.bfloat16):
    gain = block_levels(stream_key, dims, shards, -0.22, 0.18) if shards else 1.0
    values = jax.random.normal(stream_key, dims, jnp.float32) * spread * gain
    return jnp.minimum(jnp.maximum(values, -limit), limit).astype(kind)


def setup_inputs(seed: int = 0) -> dict:
    arg_keys = jax.random.split(jax.random.key(seed), 6)
    return {
        "qkv_proj": scatter_about(arg_keys[0], (3, GROUPS, GROUP, D), 1.0, 6.0, ((2, 32),)),
        "conv_kernel": scatter_about(arg_keys[1], (3, KW, D), 0.5, 3.0, (), jnp.float32),
        "qk_gain": jnp.clip(jnp.exp(math.log(2.5) - 1.8325814 * jax.random.uniform(arg_keys[2], (2, HEADS, HEAD), jnp.float32) ** block_levels(arg_keys[2], (2, HEADS, HEAD), ((1, 8),), -0.2, 0.2)), 0.4, 2.5),
        "fast_init": scatter_about(arg_keys[3], (3, HEADS, HEAD, HEAD), HEAD ** -0.5, 0.25, ((1, 8),), jnp.float32),
        "step_size": jnp.clip(jnp.exp(math.log(1.0) - 1.609438 * jax.random.uniform(arg_keys[4], (HEADS,), jnp.float32) ** block_levels(arg_keys[4], (HEADS,), ((0, 8),), -0.2, 0.2)), 0.2, 1.0),
    }


EPS = 1e-06
BETA = 0.6

def matmul(left, right):
    return jnp.dot(left, right, preferred_element_type=jnp.float32)

def contract_rows(left, right):
    return lax.dot_general(left, right, (((0,), (0,)), ((), ())), preferred_element_type=jnp.float32)

def contract_cols(left, right):
    return lax.dot_general(left, right, (((1,), (1,)), ((), ())), preferred_element_type=jnp.float32)

def rms_rows(values_in):
    values_in = values_in.astype(jnp.float32)
    return values_in * lax.rsqrt(lax.optimization_barrier(jnp.mean(values_in * values_in, axis=-1, keepdims=True)) + EPS)

def normalize_columns(moment):
    return moment * lax.rsqrt(lax.optimization_barrier(jnp.mean(moment * moment, axis=1, keepdims=True)) + EPS)

def local_gradients(weights, keys_in, values_in):
    narrow = weights.astype(jnp.bfloat16)
    gate_pre = matmul(keys_in, narrow[0])
    up_pre = matmul(keys_in, narrow[1])
    sigmoid_gate = jax.nn.sigmoid(gate_pre)
    gate_act = gate_pre * sigmoid_gate
    hidden = (gate_act * up_pre).astype(jnp.bfloat16)
    back_hidden = contract_cols(values_in, narrow[2])
    g_down = contract_rows(hidden, values_in)
    err_gate = (back_hidden * up_pre * sigmoid_gate * (1.0 + gate_pre * (1.0 - sigmoid_gate))).astype(jnp.bfloat16)
    err_up = (back_hidden * gate_act).astype(jnp.bfloat16)
    g_gate = contract_rows(keys_in, err_gate)
    g_up = contract_rows(keys_in, err_up)
    return jnp.stack([g_gate, g_up, g_down])

def apply_fast(weights, queries):
    narrow = weights.astype(jnp.bfloat16)
    hidden = (jax.nn.silu(matmul(queries, narrow[0])) * matmul(queries, narrow[1])).astype(jnp.bfloat16)
    return matmul(hidden, narrow[2])

def reference(qkv_proj, conv_kernel, qk_gain, fast_init, step_size):

    def conv_one(stream_pair):
        stream, kernel = stream_pair
        flat_rows = stream.reshape(GROUPS * GROUP, D)
        padded = jnp.concatenate([jnp.zeros((KW - 1, D), flat_rows.dtype), flat_rows], axis=0)
        summed = jnp.zeros((GROUPS * GROUP, D), jnp.float32)
        for tap_index in range(KW):
            begin = KW - 1 - tap_index
            summed = summed + kernel[tap_index] * padded[begin:begin + GROUPS * GROUP].astype(jnp.float32)
        return jax.nn.silu(summed).astype(jnp.bfloat16).reshape(GROUPS, GROUP, D)
    activated = lax.map(conv_one, (qkv_proj, conv_kernel))

    def one_head(inputs_tuple):
        head_index, gains, weights, learn_rate = inputs_tuple
        group_data = lax.dynamic_slice_in_dim(activated, head_index * HEAD, HEAD, 3)
        step_scale = learn_rate * HEAD ** (-0.5)
        momentum = jnp.zeros_like(weights)
        outputs = []
        for group_index in range(GROUPS):
            queries = (rms_rows(group_data[0, group_index]) * gains[0]).astype(jnp.bfloat16)
            keys_in = (rms_rows(group_data[1, group_index]) * gains[1]).astype(jnp.bfloat16)
            values_in = group_data[2, group_index] * (-1.0 / GROUP)
            gradients = local_gradients(weights, keys_in, values_in)
            momentum = BETA * momentum + gradients
            weights = weights - step_scale * normalize_columns(momentum)
            outputs.append(apply_fast(weights, queries))
        return jnp.stack(outputs)
    per_head = lax.map(one_head, (jnp.arange(HEADS, dtype=jnp.int32), jnp.transpose(qk_gain, (1, 0, 2)), jnp.transpose(fast_init, (1, 0, 2, 3)), step_size))
    return jnp.transpose(per_head, (1, 2, 0, 3)).reshape(GROUPS, GROUP, D).astype(jnp.bfloat16)
```

```python
import functools

import jax
import jax.numpy as jnp
from jax import lax
from jax.experimental import pallas as pl
from jax.experimental.pallas import tpu as pltpu
from jax.sharding import PartitionSpec as P

EPS = 1e-06
BETA = 0.6
RIM = 16
MESH = pl.DeviceIdType.MESH


def dot(left, right, left_dim=1, right_dim=0):
    return lax.dot_general(
        left,
        right,
        (((left_dim,), (right_dim,)), ((), ())),
        preferred_element_type=jnp.float32,
    )


def sigmoid(v):
    return 0.5 * jnp.tanh(0.5 * v) + 0.5


def silu(v):
    half = 0.5 * v
    return half * jnp.tanh(half) + half


def rms(v, gain):
    v = v.astype(jnp.float32)
    scale = lax.rsqrt(jnp.mean(v * v, axis=-1, keepdims=True) + EPS)
    return (v * scale * gain).astype(jnp.bfloat16)


def kernel(
    seq_count,
    wide_count,
    qkv,
    taps_ref,
    gain_ref,
    init_ref,
    step_ref,
    out_ref,
    raw,
    keys,
    values,
    queries,
    mids,
    weights,
    narrow,
    moment,
    pair_out,
    pair_in,
    half_sum,
    chip_out,
    chip_in,
    a2a_send,
    a2a_recv,
    rim_send,
    rim_recv,
    pair_send,
    pair_recv,
    chip_send,
    chip_recv,
    wide_send,
    wide_recv,
    init_sem,
):
    group_count, row_count = qkv.shape[1], qkv.shape[2]
    tap_count = taps_ref.shape[1]
    head = init_ref.shape[-1]
    half = head // 2
    tokens = row_count * wide_count
    group_total = tokens * seq_count
    chip_count = seq_count // 2
    seq, wide = lax.axis_index("seq"), lax.axis_index("wide")
    core, chip = lax.rem(seq, 2), seq // 2
    partner = 2 * chip + (1 - core)
    block = min(256, tokens)

    barrier = pltpu.get_barrier_semaphore()
    for d in range(1, wide_count):
        pl.semaphore_signal(
            barrier, inc=1, device_id=(seq, lax.rem(wide + d, wide_count)), device_id_type=MESH
        )
    for d in range(1, seq_count):
        pl.semaphore_signal(
            barrier, inc=1, device_id=(lax.rem(seq + d, seq_count), wide), device_id_type=MESH
        )
    pl.semaphore_wait(barrier, wide_count + seq_count - 2)

    phases = [(1, 2, g) for g in range(group_count)] + [(0, 1, g) for g in range(group_count)]

    def head_cols(h):
        return pl.ds(pl.multiple_of(h * head, head), head)

    def chunk_rows(w):
        return pl.ds(pl.multiple_of(RIM + w * row_count, RIM), row_count)

    def regroup_copy(phase, d):
        first, count, g = phases[phase]
        target = lax.rem(wide + d, wide_count)
        return pltpu.make_async_remote_copy(
            src_ref=qkv.at[pl.ds(first, count), g, :, head_cols(target)],
            dst_ref=raw.at[pl.ds(first, count), g, chunk_rows(wide), :],
            send_sem=a2a_send.at[phase, d],
            recv_sem=a2a_recv.at[phase, wide],
            device_id=(seq, target),
            device_id_type=MESH,
        )

    def start_regroup(phase):
        first, count, g = phases[phase]
        for d in range(1, wide_count):
            regroup_copy(phase, d).start()
        pltpu.make_async_copy(
            qkv.at[pl.ds(first, count), g, :, head_cols(wide)],
            raw.at[pl.ds(first, count), g, chunk_rows(wide), :],
            a2a_recv.at[phase, wide],
        ).start()

    def end_regroup(phase):
        for d in range(1, wide_count):
            regroup_copy(phase, d).wait_send()

    def wait_chunk(phase, w):
        first, count, g = phases[phase]
        pltpu.make_async_copy(
            qkv.at[pl.ds(first, count), g, :, head_cols(wide)],
            raw.at[pl.ds(first, count), g, chunk_rows(w), :],
            a2a_recv.at[phase, w],
        ).wait()

    def rim_copy(phase):
        first, count, g = phases[phase]
        wraps = (seq + 1) // seq_count
        to_group = jnp.minimum(g + wraps, group_count - 1)
        return pltpu.make_async_remote_copy(
            src_ref=raw.at[pl.ds(first, count), g, pl.ds(tokens, RIM), :],
            dst_ref=raw.at[pl.ds(first, count), to_group, pl.ds(0, RIM), :],
            send_sem=rim_send.at[phase],
            recv_sem=rim_recv.at[phase - g + to_group],
            device_id=(lax.rem(seq + 1, seq_count), wide),
            device_id_type=MESH,
        )

    def wait_rim(phase):
        first, count, g = phases[phase]
        pltpu.make_async_copy(
            raw.at[pl.ds(first, count), g, pl.ds(tokens, RIM), :],
            raw.at[pl.ds(first, count), g, pl.ds(0, RIM), :],
            rim_recv.at[phase],
        ).wait()

    def rim_sends(phase, act):
        if phases[phase][2] == group_count - 1:
            pl.when(seq < seq_count - 1)(act)
        else:
            act()

    def conv_chunk(phase, w):
        first, count, g = phases[phase]
        base = pl.multiple_of(w * row_count, RIM)
        for stream in range(first, first + count):
            rows = raw[stream, g, pl.ds(base, RIM + row_count), :].astype(jnp.float32)
            taps = taps_ref[stream, :, head_cols(wide)]
            summed = taps[0:1] * rows[RIM : RIM + row_count]
            for j in range(1, tap_count):
                summed = summed + taps[j : j + 1] * rows[RIM - j : RIM - j + row_count]
            activated = silu(summed).astype(jnp.bfloat16)
            at = pl.ds(base, row_count)
            if stream == 0:
                queries[at, :] = rms(activated, gain_ref[0])
            elif stream == 1:
                keys[at, :] = rms(activated, gain_ref[1])
            else:
                values[at, :] = (activated.astype(jnp.float32) * (-1.0 / group_total)).astype(
                    jnp.bfloat16
                )

    def convolve(phase):
        wait_chunk(phase, 0)
        wait_chunk(phase, wide_count - 1)
        rim_sends(phase, lambda: rim_copy(phase).start())

        def body(w, carry):
            wait_chunk(phase, w)
            conv_chunk(phase, w)
            return carry

        lax.fori_loop(1, wide_count - 1, body, 0)
        conv_chunk(phase, wide_count - 1)
        if phases[phase][2] == 0:
            pl.when(seq > 0)(lambda: wait_rim(phase))
        else:
            wait_rim(phase)
        conv_chunk(phase, 0)

    def pair_copy(g, m):
        return pltpu.make_async_remote_copy(
            src_ref=pair_out.at[g, m],
            dst_ref=pair_in.at[g, m],
            send_sem=pair_send.at[g, m],
            recv_sem=pair_recv.at[g, m],
            device_id=(partner, wide),
            device_id_type=MESH,
        )

    def chip_copy(g, m, d):
        other = 2 * lax.rem(chip + d, chip_count) + core
        return pltpu.make_async_remote_copy(
            src_ref=chip_out.at[g, m],
            dst_ref=chip_in.at[g, m, d - 1],
            send_sem=chip_send.at[g, m, d - 1],
            recv_sem=chip_recv.at[g, m, d - 1],
            device_id=(other, wide),
            device_id_type=MESH,
        )

    own_cols = pl.ds(pl.multiple_of(core * half, half), half)
    other_cols = pl.ds(pl.multiple_of((1 - core) * half, half), half)

    def weight_copy(g, m, cols):
        return pltpu.make_async_remote_copy(
            src_ref=narrow.at[g + 1, m, :, cols],
            dst_ref=narrow.at[g + 1, m, :, cols],
            send_sem=wide_send.at[g, m],
            recv_sem=wide_recv.at[g, m],
            device_id=(partner, wide),
            device_id_type=MESH,
        )

    def gradients(g):
        for t in range(tokens // block):
            at = pl.ds(t * block, block)
            a = dot(keys[at, :], narrow[g, 0])
            b = dot(keys[at, :], narrow[g, 1])
            sg = sigmoid(a)
            act = a * sg
            mids[2, at, :] = (act * b).astype(jnp.bfloat16)
            back = dot(values[at, :], narrow[g, 2], 1, 1)
            mids[0, at, :] = (back * b * sg * (1.0 + a * (1.0 - sg))).astype(jnp.bfloat16)
            mids[1, at, :] = (back * act).astype(jnp.bfloat16)

        def part(m, cols):
            if m == 2:
                return dot(mids[2], values[:, cols], 0, 0)
            return dot(keys[...], mids[m, :, cols], 0, 0)

        for m in (2, 0, 1):
            pair_out[g, m] = part(m, other_cols).astype(jnp.bfloat16)
            pair_copy(g, m).start()
        for m in (2, 0, 1):
            half_sum[m] = part(m, own_cols)
            pair_copy(g, m).wait_recv()
            total = half_sum[m] + pair_in[g, m].astype(jnp.float32)
            half_sum[m] = total
            if chip_count > 1:
                chip_out[g, m] = total.astype(jnp.bfloat16)
                for d in range(1, chip_count):
                    chip_copy(g, m, d).start()

    def update(g):
        scale = step_ref[...] * head ** (-0.5)
        for m in (2, 0, 1):
            total = half_sum[m]
            for d in range(1, chip_count):
                chip_copy(g, m, d).wait_recv()
                total = total + chip_in[g, m, d - 1].astype(jnp.float32)
            if g > 0:
                total = BETA * moment[m] + total
            moment[m] = total
            norm = lax.rsqrt(jnp.mean(total * total, axis=0, keepdims=True) + EPS)
            new = weights[m, :, own_cols] - scale * (total * norm)
            weights[m, :, own_cols] = new
            narrow[g + 1, m, :, own_cols] = new.astype(jnp.bfloat16)
            weight_copy(g, m, own_cols).start()
        for m in (2, 0, 1):
            weight_copy(g, m, other_cols).wait_recv()

    def apply(g):
        for t in range(tokens // block):
            at = pl.ds(t * block, block)
            a = dot(queries[at, :], narrow[g + 1, 0])
            b = dot(queries[at, :], narrow[g + 1, 1])
            p = (silu(a) * b).astype(jnp.bfloat16)
            out_ref[g, at, :] = dot(p, narrow[g + 1, 2]).astype(jnp.bfloat16)

    load = pltpu.make_async_copy(init_ref.at[:, 0], weights, init_sem)
    start_regroup(0)
    load.start()

    @pl.when(seq == 0)
    def _():
        for stream in range(3):
            raw[stream, 0, 0:RIM, :] = jnp.zeros((RIM, head), jnp.bfloat16)

    load.wait()
    for m in range(3):
        narrow[0, m] = weights[m].astype(jnp.bfloat16)

    for g in range(group_count):
        convolve(g)
        end_regroup(g)
        if g + 1 < group_count:
            start_regroup(g + 1)
        else:
            for later in range(group_count):
                start_regroup(group_count + later)
        if g > 0:
            update(g - 1)
        gradients(g)
    for g in range(group_count):
        convolve(group_count + g)
        if g == group_count - 1:
            update(g)
        apply(g)

    for phase in range(2 * group_count):
        if phase >= group_count:
            end_regroup(phase)
        rim_sends(phase, lambda phase=phase: rim_copy(phase).wait_send())
    for g in range(group_count):
        for m in range(3):
            pair_copy(g, m).wait_send()
            weight_copy(g, m, own_cols).wait_send()
            for d in range(1, chip_count):
                chip_copy(g, m, d).wait_send()


def local(qkv_proj, conv_kernel, qk_gain, fast_init, step_size):
    seq_count, wide_count = lax.axis_size("seq"), lax.axis_size("wide")
    group_count, row_count = qkv_proj.shape[1:3]
    head = fast_init.shape[-1]
    half = head // 2
    tokens = row_count * wide_count
    chip_slots = max(1, seq_count // 2 - 1)
    wide_type, full_type = jnp.bfloat16, jnp.float32
    vmem = pl.BlockSpec(memory_space=pltpu.VMEM)
    hbm = pl.BlockSpec(memory_space=pl.ANY)
    dma = pltpu.SemaphoreType.DMA
    matmuls = group_count * 9
    return pl.pallas_call(
        functools.partial(kernel, seq_count, wide_count),
        out_shape=jax.ShapeDtypeStruct((group_count, tokens, head), wide_type),
        in_specs=[hbm, vmem, vmem, hbm, vmem],
        out_specs=vmem,
        scratch_shapes=[
            pltpu.VMEM((3, group_count, RIM + tokens, head), wide_type),
            pltpu.VMEM((tokens, head), wide_type),
            pltpu.VMEM((tokens, head), wide_type),
            pltpu.VMEM((tokens, head), wide_type),
            pltpu.VMEM((3, tokens, head), wide_type),
            pltpu.VMEM((3, head, head), full_type),
            pltpu.VMEM((group_count + 1, 3, head, head), wide_type),
            pltpu.VMEM((3, head, half), full_type),
            pltpu.VMEM((group_count, 3, head, half), wide_type),
            pltpu.VMEM((group_count, 3, head, half), wide_type),
            pltpu.VMEM((3, head, half), full_type),
            pltpu.VMEM((group_count, 3, head, half), wide_type),
            pltpu.VMEM((group_count, 3, chip_slots, head, half), wide_type),
            dma((2 * group_count, wide_count)),
            dma((2 * group_count, wide_count)),
            dma((2 * group_count,)),
            dma((2 * group_count,)),
            dma((group_count, 3)),
            dma((group_count, 3)),
            dma((group_count, 3, chip_slots)),
            dma((group_count, 3, chip_slots)),
            dma((group_count, 3)),
            dma((group_count, 3)),
            dma(()),
        ],
        compiler_params=pltpu.CompilerParams(
            collective_id=0, has_side_effects=True, vmem_limit_bytes=56 * 1024 * 1024
        ),
        cost_estimate=pl.CostEstimate(
            flops=matmuls * 2 * tokens * head * head,
            bytes_accessed=2 * qkv_proj.size,
            transcendentals=qkv_proj.size,
        ),
    )(qkv_proj, conv_kernel, qk_gain, fast_init, step_size.reshape(1, 1))


def solution(mesh):
    in_specs = (
        P(None, None, ("seq", "wide"), None),
        P(),
        P(None, "wide", None),
        P(None, "wide", None, None),
        P("wide"),
    )
    out_specs = P(None, "seq", "wide")
    return jax.shard_map(local, mesh=mesh, in_specs=in_specs, out_specs=out_specs, check_vma=False)
```

```python
import functools

import jax
import jax.numpy as jnp
from jax import lax
from jax.experimental import pallas as pl
from jax.experimental.pallas import tpu as pltpu
from jax.sharding import PartitionSpec as P

EPS = 1e-06
BETA = 0.6
RIM = 16
MESH = pl.DeviceIdType.MESH


def dot(left, right, left_dim=1, right_dim=0):
    return lax.dot_general(
        left,
        right,
        (((left_dim,), (right_dim,)), ((), ())),
        preferred_element_type=jnp.float32,
    )


def sigmoid(v):
    return 0.5 * jnp.tanh(0.5 * v) + 0.5


def silu(v):
    half = 0.5 * v
    return half * jnp.tanh(half) + half


def rms(v, gain):
    v = v.astype(jnp.float32)
    scale = lax.rsqrt(jnp.mean(v * v, axis=-1, keepdims=True) + EPS)
    return (v * scale * gain).astype(jnp.bfloat16)


def kernel(
    seq_count,
    wide_count,
    qkv,
    taps_ref,
    gain_ref,
    init_ref,
    step_ref,
    out_ref,
    raw,
    keys,
    values,
    queries,
    mids,
    weights,
    narrow,
    moment,
    pair_out,
    pair_in,
    half_sum,
    chip_out,
    chip_in,
    a2a_send,
    a2a_recv,
    rim_send,
    rim_recv,
    pair_send,
    pair_recv,
    chip_send,
    chip_recv,
    wide_send,
    wide_recv,
    init_sem,
):
    group_count, row_count = qkv.shape[1], qkv.shape[2]
    tap_count = taps_ref.shape[1]
    head = init_ref.shape[-1]
    half = head // 2
    tokens = row_count * wide_count
    group_total = tokens * seq_count
    chip_count = seq_count // 2
    seq, wide = lax.axis_index("seq"), lax.axis_index("wide")
    core, chip = lax.rem(seq, 2), seq // 2
    partner = 2 * chip + (1 - core)
    block = min(256, tokens)

    barrier = pltpu.get_barrier_semaphore()
    for d in range(1, wide_count):
        pl.semaphore_signal(
            barrier, inc=1, device_id=(seq, lax.rem(wide + d, wide_count)), device_id_type=MESH
        )
    for d in range(1, seq_count):
        pl.semaphore_signal(
            barrier, inc=1, device_id=(lax.rem(seq + d, seq_count), wide), device_id_type=MESH
        )
    pl.semaphore_wait(barrier, wide_count + seq_count - 2)

    phases = [(1, 2, g) for g in range(group_count)] + [(0, 1, g) for g in range(group_count)]

    def head_cols(h):
        return pl.ds(pl.multiple_of(h * head, head), head)

    def chunk_rows(w):
        return pl.ds(pl.multiple_of(RIM + w * row_count, RIM), row_count)

    def regroup_copy(phase, d):
        first, count, g = phases[phase]
        target = lax.rem(wide + d, wide_count)
        return pltpu.make_async_remote_copy(
            src_ref=qkv.at[pl.ds(first, count), g, :, head_cols(target)],
            dst_ref=raw.at[pl.ds(first, count), g, chunk_rows(wide), :],
            send_sem=a2a_send.at[phase, d],
            recv_sem=a2a_recv.at[phase, wide],
            device_id=(seq, target),
            device_id_type=MESH,
        )

    def start_regroup(phase):
        first, count, g = phases[phase]
        for d in range(1, wide_count):
            regroup_copy(phase, d).start()
        pltpu.make_async_copy(
            qkv.at[pl.ds(first, count), g, :, head_cols(wide)],
            raw.at[pl.ds(first, count), g, chunk_rows(wide), :],
            a2a_recv.at[phase, wide],
        ).start()

    def end_regroup(phase):
        for d in range(1, wide_count):
            regroup_copy(phase, d).wait_send()

    def wait_chunk(phase, w):
        first, count, g = phases[phase]
        pltpu.make_async_copy(
            qkv.at[pl.ds(first, count), g, :, head_cols(wide)],
            raw.at[pl.ds(first, count), g, chunk_rows(w), :],
            a2a_recv.at[phase, w],
        ).wait()

    def rim_copy(phase):
        first, count, g = phases[phase]
        wraps = (seq + 1) // seq_count
        to_group = jnp.minimum(g + wraps, group_count - 1)
        return pltpu.make_async_remote_copy(
            src_ref=raw.at[pl.ds(first, count), g, pl.ds(tokens, RIM), :],
            dst_ref=raw.at[pl.ds(first, count), to_group, pl.ds(0, RIM), :],
            send_sem=rim_send.at[phase],
            recv_sem=rim_recv.at[phase - g + to_group],
            device_id=(lax.rem(seq + 1, seq_count), wide),
            device_id_type=MESH,
        )

    def wait_rim(phase):
        first, count, g = phases[phase]
        pltpu.make_async_copy(
            raw.at[pl.ds(first, count), g, pl.ds(tokens, RIM), :],
            raw.at[pl.ds(first, count), g, pl.ds(0, RIM), :],
            rim_recv.at[phase],
        ).wait()

    def rim_sends(phase, act):
        if phases[phase][2] == group_count - 1:
            pl.when(seq < seq_count - 1)(act)
        else:
            act()

    def conv_chunk(phase, w):
        first, count, g = phases[phase]
        base = pl.multiple_of(w * row_count, RIM)
        for stream in range(first, first + count):
            rows = raw[stream, g, pl.ds(base, RIM + row_count), :].astype(jnp.float32)
            taps = taps_ref[stream, :, head_cols(wide)]
            summed = taps[0:1] * rows[RIM : RIM + row_count]
            for j in range(1, tap_count):
                summed = summed + taps[j : j + 1] * rows[RIM - j : RIM - j + row_count]
            activated = silu(summed).astype(jnp.bfloat16)
            at = pl.ds(base, row_count)
            if stream == 0:
                queries[at, :] = rms(activated, gain_ref[0])
            elif stream == 1:
                keys[at, :] = rms(activated, gain_ref[1])
            else:
                values[at, :] = (activated.astype(jnp.float32) * (-1.0 / group_total)).astype(
                    jnp.bfloat16
                )

    def convolve(phase):
        wait_chunk(phase, 0)
        wait_chunk(phase, wide_count - 1)
        rim_sends(phase, lambda: rim_copy(phase).start())

        def body(w, carry):
            wait_chunk(phase, w)
            conv_chunk(phase, w)
            return carry

        lax.fori_loop(1, wide_count - 1, body, 0)
        conv_chunk(phase, wide_count - 1)
        if phases[phase][2] == 0:
            pl.when(seq > 0)(lambda: wait_rim(phase))
        else:
            wait_rim(phase)
        conv_chunk(phase, 0)

    def pair_copy(g, m):
        return pltpu.make_async_remote_copy(
            src_ref=pair_out.at[g, m],
            dst_ref=pair_in.at[g, m],
            send_sem=pair_send.at[g, m],
            recv_sem=pair_recv.at[g, m],
            device_id=(partner, wide),
            device_id_type=MESH,
        )

    def chip_copy(g, m, d):
        other = 2 * lax.rem(chip + d, chip_count) + core
        return pltpu.make_async_remote_copy(
            src_ref=chip_out.at[g, m],
            dst_ref=chip_in.at[g, m, d - 1],
            send_sem=chip_send.at[g, m, d - 1],
            recv_sem=chip_recv.at[g, m, d - 1],
            device_id=(other, wide),
            device_id_type=MESH,
        )

    own_cols = pl.ds(pl.multiple_of(core * half, half), half)
    other_cols = pl.ds(pl.multiple_of((1 - core) * half, half), half)

    def weight_copy(g, m, cols):
        return pltpu.make_async_remote_copy(
            src_ref=narrow.at[g + 1, m, :, cols],
            dst_ref=narrow.at[g + 1, m, :, cols],
            send_sem=wide_send.at[g, m],
            recv_sem=wide_recv.at[g, m],
            device_id=(partner, wide),
            device_id_type=MESH,
        )

    def gradients(g):
        for t in range(tokens // block):
            at = pl.ds(t * block, block)
            a = dot(keys[at, :], narrow[g, 0])
            b = dot(keys[at, :], narrow[g, 1])
            sg = sigmoid(a)
            act = a * sg
            mids[2, at, :] = (act * b).astype(jnp.bfloat16)
            back = dot(values[at, :], narrow[g, 2], 1, 1)
            mids[0, at, :] = (back * b * sg * (1.0 + a * (1.0 - sg))).astype(jnp.bfloat16)
            mids[1, at, :] = (back * act).astype(jnp.bfloat16)

        def part(m, cols):
            if m == 2:
                return dot(mids[2], values[:, cols], 0, 0)
            return dot(keys[...], mids[m, :, cols], 0, 0)

        for m in (2, 0, 1):
            pair_out[g, m] = part(m, other_cols).astype(jnp.bfloat16)
            pair_copy(g, m).start()
        for m in (2, 0, 1):
            half_sum[m] = part(m, own_cols)
            pair_copy(g, m).wait_recv()
            total = half_sum[m] + pair_in[g, m].astype(jnp.float32)
            half_sum[m] = total
            if chip_count > 1:
                chip_out[g, m] = total.astype(jnp.bfloat16)
                for d in range(1, chip_count):
                    chip_copy(g, m, d).start()

    def update(g):
        scale = step_ref[...] * head ** (-0.5)
        for m in (2, 0, 1):
            total = half_sum[m]
            for d in range(1, chip_count):
                chip_copy(g, m, d).wait_recv()
                total = total + chip_in[g, m, d - 1].astype(jnp.float32)
            if g > 0:
                total = BETA * moment[m] + total
            moment[m] = total
            norm = lax.rsqrt(jnp.mean(total * total, axis=0, keepdims=True) + EPS)
            new = weights[m, :, own_cols] - scale * (total * norm)
            weights[m, :, own_cols] = new
            narrow[g + 1, m, :, own_cols] = new.astype(jnp.bfloat16)
            weight_copy(g, m, own_cols).start()
        for m in (2, 0, 1):
            weight_copy(g, m, other_cols).wait_recv()

    def apply(g):
        for t in range(tokens // block):
            at = pl.ds(t * block, block)
            a = dot(queries[at, :], narrow[g + 1, 0])
            b = dot(queries[at, :], narrow[g + 1, 1])
            p = (silu(a) * b).astype(jnp.bfloat16)
            out_ref[g, at, :] = dot(p, narrow[g + 1, 2]).astype(jnp.bfloat16)

    load = pltpu.make_async_copy(init_ref.at[:, 0], weights, init_sem)
    start_regroup(0)
    load.start()

    @pl.when(seq == 0)
    def _():
        for stream in range(3):
            raw[stream, 0, 0:RIM, :] = jnp.zeros((RIM, head), jnp.bfloat16)

    load.wait()
    for m in range(3):
        narrow[0, m] = weights[m].astype(jnp.bfloat16)

    for g in range(group_count):
        end_regroup(g)
        if g + 1 < group_count:
            start_regroup(g + 1)
        else:
            for later in range(group_count):
                start_regroup(group_count + later)
        convolve(g)
        if g > 0:
            update(g - 1)
        gradients(g)
    for g in range(group_count):
        convolve(group_count + g)
        if g == group_count - 1:
            update(g)
        apply(g)

    for phase in range(2 * group_count):
        if phase >= group_count:
            end_regroup(phase)
        rim_sends(phase, lambda phase=phase: rim_copy(phase).wait_send())
    for g in range(group_count):
        for m in range(3):
            pair_copy(g, m).wait_send()
            weight_copy(g, m, own_cols).wait_send()
            for d in range(1, chip_count):
                chip_copy(g, m, d).wait_send()


def local(qkv_proj, conv_kernel, qk_gain, fast_init, step_size):
    seq_count, wide_count = lax.axis_size("seq"), lax.axis_size("wide")
    group_count, row_count = qkv_proj.shape[1:3]
    head = fast_init.shape[-1]
    half = head // 2
    tokens = row_count * wide_count
    chip_slots = max(1, seq_count // 2 - 1)
    wide_type, full_type = jnp.bfloat16, jnp.float32
    vmem = pl.BlockSpec(memory_space=pltpu.VMEM)
    hbm = pl.BlockSpec(memory_space=pl.ANY)
    dma = pltpu.SemaphoreType.DMA
    matmuls = group_count * 9
    return pl.pallas_call(
        functools.partial(kernel, seq_count, wide_count),
        out_shape=jax.ShapeDtypeStruct((group_count, tokens, head), wide_type),
        in_specs=[hbm, vmem, vmem, hbm, vmem],
        out_specs=vmem,
        scratch_shapes=[
            pltpu.VMEM((3, group_count, RIM + tokens, head), wide_type),
            pltpu.VMEM((tokens, head), wide_type),
            pltpu.VMEM((tokens, head), wide_type),
            pltpu.VMEM((tokens, head), wide_type),
            pltpu.VMEM((3, tokens, head), wide_type),
            pltpu.VMEM((3, head, head), full_type),
            pltpu.VMEM((group_count + 1, 3, head, head), wide_type),
            pltpu.VMEM((3, head, half), full_type),
            pltpu.VMEM((group_count, 3, head, half), wide_type),
            pltpu.VMEM((group_count, 3, head, half), wide_type),
            pltpu.VMEM((3, head, half), full_type),
            pltpu.VMEM((group_count, 3, head, half), wide_type),
            pltpu.VMEM((group_count, 3, chip_slots, head, half), wide_type),
            dma((2 * group_count, wide_count)),
            dma((2 * group_count, wide_count)),
            dma((2 * group_count,)),
            dma((2 * group_count,)),
            dma((group_count, 3)),
            dma((group_count, 3)),
            dma((group_count, 3, chip_slots)),
            dma((group_count, 3, chip_slots)),
            dma((group_count, 3)),
            dma((group_count, 3)),
            dma(()),
        ],
        compiler_params=pltpu.CompilerParams(
            collective_id=0, has_side_effects=True, vmem_limit_bytes=56 * 1024 * 1024
        ),
        cost_estimate=pl.CostEstimate(
            flops=matmuls * 2 * tokens * head * head,
            bytes_accessed=2 * qkv_proj.size,
            transcendentals=qkv_proj.size,
        ),
    )(qkv_proj, conv_kernel, qk_gain, fast_init, step_size.reshape(1, 1))


def solution(mesh):
    in_specs = (
        P(None, None, ("seq", "wide"), None),
        P(),
        P(None, "wide", None),
        P(None, "wide", None, None),
        P("wide"),
    )
    out_specs = P(None, "seq", "wide")
    return jax.shard_map(local, mesh=mesh, in_specs=in_specs, out_specs=out_specs, check_vma=False)
```

```python
import functools

import jax
import jax.numpy as jnp
from jax import lax
from jax.experimental import pallas as pl
from jax.experimental.pallas import tpu as pltpu
from jax.sharding import PartitionSpec as P

EPS = 1e-06
BETA = 0.6
RIM = 16
MESH = pl.DeviceIdType.MESH


def dot(left, right, left_dim=1, right_dim=0):
    return lax.dot_general(
        left,
        right,
        (((left_dim,), (right_dim,)), ((), ())),
        preferred_element_type=jnp.float32,
    )


def sigmoid(v):
    return 0.5 * jnp.tanh(0.5 * v) + 0.5


def silu(v):
    half = 0.5 * v
    return half * jnp.tanh(half) + half


def rms(v, gain):
    v = v.astype(jnp.float32)
    scale = lax.rsqrt(jnp.mean(v * v, axis=-1, keepdims=True) + EPS)
    return (v * scale * gain).astype(jnp.bfloat16)


def kernel(
    seq_count,
    wide_count,
    qkv,
    taps_ref,
    gain_ref,
    init_ref,
    step_ref,
    out_ref,
    raw,
    keys,
    values,
    queries,
    mids,
    weights,
    narrow,
    moment,
    pair_out,
    pair_in,
    half_sum,
    chip_out,
    chip_in,
    a2a_send,
    a2a_recv,
    rim_send,
    rim_recv,
    pair_send,
    pair_recv,
    chip_send,
    chip_recv,
    wide_send,
    wide_recv,
    init_sem,
):
    group_count, row_count = qkv.shape[1], qkv.shape[2]
    tap_count = taps_ref.shape[1]
    head = init_ref.shape[-1]
    half = head // 2
    tokens = row_count * wide_count
    group_total = tokens * seq_count
    chip_count = seq_count // 2
    seq, wide = lax.axis_index("seq"), lax.axis_index("wide")
    core, chip = lax.rem(seq, 2), seq // 2
    partner = 2 * chip + (1 - core)
    block = min(256, tokens)

    barrier = pltpu.get_barrier_semaphore()
    for d in range(1, wide_count):
        pl.semaphore_signal(
            barrier, inc=1, device_id=(seq, lax.rem(wide + d, wide_count)), device_id_type=MESH
        )
    for d in range(1, seq_count):
        pl.semaphore_signal(
            barrier, inc=1, device_id=(lax.rem(seq + d, seq_count), wide), device_id_type=MESH
        )
    pl.semaphore_wait(barrier, wide_count + seq_count - 2)

    phases = [(1, 2, g) for g in range(group_count)] + [(0, 1, g) for g in range(group_count)]

    def head_cols(h):
        return pl.ds(pl.multiple_of(h * head, head), head)

    def chunk_rows(w):
        return pl.ds(pl.multiple_of(RIM + w * row_count, RIM), row_count)

    def regroup_copy(phase, d):
        first, count, g = phases[phase]
        target = lax.rem(wide + d, wide_count)
        return pltpu.make_async_remote_copy(
            src_ref=qkv.at[pl.ds(first, count), g, :, head_cols(target)],
            dst_ref=raw.at[pl.ds(first, count), g, chunk_rows(wide), :],
            send_sem=a2a_send.at[phase, d],
            recv_sem=a2a_recv.at[phase, wide],
            device_id=(seq, target),
            device_id_type=MESH,
        )

    def start_regroup(phase):
        first, count, g = phases[phase]
        for d in sorted(range(1, wide_count), key=lambda d: abs(d - wide_count // 2)):
            regroup_copy(phase, d).start()
        pltpu.make_async_copy(
            qkv.at[pl.ds(first, count), g, :, head_cols(wide)],
            raw.at[pl.ds(first, count), g, chunk_rows(wide), :],
            a2a_recv.at[phase, wide],
        ).start()

    def end_regroup(phase):
        for d in range(1, wide_count):
            regroup_copy(phase, d).wait_send()

    def wait_chunk(phase, w):
        first, count, g = phases[phase]
        pltpu.make_async_copy(
            qkv.at[pl.ds(first, count), g, :, head_cols(wide)],
            raw.at[pl.ds(first, count), g, chunk_rows(w), :],
            a2a_recv.at[phase, w],
        ).wait()

    def rim_copy(phase):
        first, count, g = phases[phase]
        wraps = (seq + 1) // seq_count
        to_group = jnp.minimum(g + wraps, group_count - 1)
        return pltpu.make_async_remote_copy(
            src_ref=raw.at[pl.ds(first, count), g, pl.ds(tokens, RIM), :],
            dst_ref=raw.at[pl.ds(first, count), to_group, pl.ds(0, RIM), :],
            send_sem=rim_send.at[phase],
            recv_sem=rim_recv.at[phase - g + to_group],
            device_id=(lax.rem(seq + 1, seq_count), wide),
            device_id_type=MESH,
        )

    def wait_rim(phase):
        first, count, g = phases[phase]
        pltpu.make_async_copy(
            raw.at[pl.ds(first, count), g, pl.ds(tokens, RIM), :],
            raw.at[pl.ds(first, count), g, pl.ds(0, RIM), :],
            rim_recv.at[phase],
        ).wait()

    def rim_sends(phase, act):
        if phases[phase][2] == group_count - 1:
            pl.when(seq < seq_count - 1)(act)
        else:
            act()

    def conv_chunk(phase, w):
        first, count, g = phases[phase]
        base = pl.multiple_of(w * row_count, RIM)
        for stream in range(first, first + count):
            rows = raw[stream, g, pl.ds(base, RIM + row_count), :].astype(jnp.float32)
            taps = taps_ref[stream, :, head_cols(wide)]
            summed = taps[0:1] * rows[RIM : RIM + row_count]
            for j in range(1, tap_count):
                summed = summed + taps[j : j + 1] * rows[RIM - j : RIM - j + row_count]
            activated = silu(summed).astype(jnp.bfloat16)
            at = pl.ds(base, row_count)
            if stream == 0:
                queries[at, :] = rms(activated, gain_ref[0])
            elif stream == 1:
                keys[at, :] = rms(activated, gain_ref[1])
            else:
                values[at, :] = (activated.astype(jnp.float32) * (-1.0 / group_total)).astype(
                    jnp.bfloat16
                )

    def convolve(phase):
        wait_chunk(phase, 0)
        wait_chunk(phase, wide_count - 1)
        rim_sends(phase, lambda: rim_copy(phase).start())

        def body(w, carry):
            wait_chunk(phase, w)
            conv_chunk(phase, w)
            return carry

        lax.fori_loop(1, wide_count - 1, body, 0)
        conv_chunk(phase, wide_count - 1)
        if phases[phase][2] == 0:
            pl.when(seq > 0)(lambda: wait_rim(phase))
        else:
            wait_rim(phase)
        conv_chunk(phase, 0)

    def pair_copy(g, m):
        return pltpu.make_async_remote_copy(
            src_ref=pair_out.at[g, m],
            dst_ref=pair_in.at[g, m],
            send_sem=pair_send.at[g, m],
            recv_sem=pair_recv.at[g, m],
            device_id=(partner, wide),
            device_id_type=MESH,
        )

    def chip_copy(g, m, d):
        other = 2 * lax.rem(chip + d, chip_count) + core
        return pltpu.make_async_remote_copy(
            src_ref=chip_out.at[g, m],
            dst_ref=chip_in.at[g, m, d - 1],
            send_sem=chip_send.at[g, m, d - 1],
            recv_sem=chip_recv.at[g, m, d - 1],
            device_id=(other, wide),
            device_id_type=MESH,
        )

    own_cols = pl.ds(pl.multiple_of(core * half, half), half)
    other_cols = pl.ds(pl.multiple_of((1 - core) * half, half), half)

    def weight_copy(g, m, cols):
        return pltpu.make_async_remote_copy(
            src_ref=narrow.at[g + 1, m, :, cols],
            dst_ref=narrow.at[g + 1, m, :, cols],
            send_sem=wide_send.at[g, m],
            recv_sem=wide_recv.at[g, m],
            device_id=(partner, wide),
            device_id_type=MESH,
        )

    def gradients(g):
        for t in range(tokens // block):
            at = pl.ds(t * block, block)
            a = dot(keys[at, :], narrow[g, 0])
            b = dot(keys[at, :], narrow[g, 1])
            sg = sigmoid(a)
            act = a * sg
            mids[2, at, :] = (act * b).astype(jnp.bfloat16)
            back = dot(values[at, :], narrow[g, 2], 1, 1)
            mids[0, at, :] = (back * b * sg * (1.0 + a * (1.0 - sg))).astype(jnp.bfloat16)
            mids[1, at, :] = (back * act).astype(jnp.bfloat16)

        def part(m, cols):
            if m == 2:
                return dot(mids[2], values[:, cols], 0, 0)
            return dot(keys[...], mids[m, :, cols], 0, 0)

        for m in (2, 0, 1):
            pair_out[g, m] = part(m, other_cols).astype(jnp.bfloat16)
            pair_copy(g, m).start()
        for m in (2, 0, 1):
            half_sum[m] = part(m, own_cols)
            pair_copy(g, m).wait_recv()
            total = half_sum[m] + pair_in[g, m].astype(jnp.float32)
            half_sum[m] = total
            if chip_count > 1:
                chip_out[g, m] = total.astype(jnp.bfloat16)
                for d in range(1, chip_count):
                    chip_copy(g, m, d).start()

    def update(g):
        scale = step_ref[...] * head ** (-0.5)
        for m in (2, 0, 1):
            total = half_sum[m]
            for d in range(1, chip_count):
                chip_copy(g, m, d).wait_recv()
                total = total + chip_in[g, m, d - 1].astype(jnp.float32)
            if g > 0:
                total = BETA * moment[m] + total
            moment[m] = total
            norm = lax.rsqrt(jnp.mean(total * total, axis=0, keepdims=True) + EPS)
            new = weights[m, :, own_cols] - scale * (total * norm)
            weights[m, :, own_cols] = new
            narrow[g + 1, m, :, own_cols] = new.astype(jnp.bfloat16)
            weight_copy(g, m, own_cols).start()
        for m in (2, 0, 1):
            weight_copy(g, m, other_cols).wait_recv()

    def apply(g):
        for t in range(tokens // block):
            at = pl.ds(t * block, block)
            a = dot(queries[at, :], narrow[g + 1, 0])
            b = dot(queries[at, :], narrow[g + 1, 1])
            p = (silu(a) * b).astype(jnp.bfloat16)
            out_ref[g, at, :] = dot(p, narrow[g + 1, 2]).astype(jnp.bfloat16)

    load = pltpu.make_async_copy(init_ref.at[:, 0], weights, init_sem)
    start_regroup(0)
    load.start()

    @pl.when(seq == 0)
    def _():
        for stream in range(3):
            raw[stream, 0, 0:RIM, :] = jnp.zeros((RIM, head), jnp.bfloat16)

    load.wait()
    for m in range(3):
        narrow[0, m] = weights[m].astype(jnp.bfloat16)

    for g in range(group_count):
        convolve(g)
        end_regroup(g)
        if g + 1 < group_count:
            start_regroup(g + 1)
        else:
            for later in range(group_count):
                start_regroup(group_count + later)
        if g > 0:
            update(g - 1)
        gradients(g)
    for g in range(group_count):
        convolve(group_count + g)
        if g == group_count - 1:
            update(g)
        apply(g)

    for phase in range(2 * group_count):
        if phase >= group_count:
            end_regroup(phase)
        rim_sends(phase, lambda phase=phase: rim_copy(phase).wait_send())
    for g in range(group_count):
        for m in range(3):
            pair_copy(g, m).wait_send()
            weight_copy(g, m, own_cols).wait_send()
            for d in range(1, chip_count):
                chip_copy(g, m, d).wait_send()


def local(qkv_proj, conv_kernel, qk_gain, fast_init, step_size):
    seq_count, wide_count = lax.axis_size("seq"), lax.axis_size("wide")
    group_count, row_count = qkv_proj.shape[1:3]
    head = fast_init.shape[-1]
    half = head // 2
    tokens = row_count * wide_count
    chip_slots = max(1, seq_count // 2 - 1)
    wide_type, full_type = jnp.bfloat16, jnp.float32
    vmem = pl.BlockSpec(memory_space=pltpu.VMEM)
    hbm = pl.BlockSpec(memory_space=pl.ANY)
    dma = pltpu.SemaphoreType.DMA
    matmuls = group_count * 9
    return pl.pallas_call(
        functools.partial(kernel, seq_count, wide_count),
        out_shape=jax.ShapeDtypeStruct((group_count, tokens, head), wide_type),
        in_specs=[hbm, vmem, vmem, hbm, vmem],
        out_specs=vmem,
        scratch_shapes=[
            pltpu.VMEM((3, group_count, RIM + tokens, head), wide_type),
            pltpu.VMEM((tokens, head), wide_type),
            pltpu.VMEM((tokens, head), wide_type),
            pltpu.VMEM((tokens, head), wide_type),
            pltpu.VMEM((3, tokens, head), wide_type),
            pltpu.VMEM((3, head, head), full_type),
            pltpu.VMEM((group_count + 1, 3, head, head), wide_type),
            pltpu.VMEM((3, head, half), full_type),
            pltpu.VMEM((group_count, 3, head, half), wide_type),
            pltpu.VMEM((group_count, 3, head, half), wide_type),
            pltpu.VMEM((3, head, half), full_type),
            pltpu.VMEM((group_count, 3, head, half), wide_type),
            pltpu.VMEM((group_count, 3, chip_slots, head, half), wide_type),
            dma((2 * group_count, wide_count)),
            dma((2 * group_count, wide_count)),
            dma((2 * group_count,)),
            dma((2 * group_count,)),
            dma((group_count, 3)),
            dma((group_count, 3)),
            dma((group_count, 3, chip_slots)),
            dma((group_count, 3, chip_slots)),
            dma((group_count, 3)),
            dma((group_count, 3)),
            dma(()),
        ],
        compiler_params=pltpu.CompilerParams(
            collective_id=0, has_side_effects=True, vmem_limit_bytes=56 * 1024 * 1024
        ),
        cost_estimate=pl.CostEstimate(
            flops=matmuls * 2 * tokens * head * head,
            bytes_accessed=2 * qkv_proj.size,
            transcendentals=qkv_proj.size,
        ),
    )(qkv_proj, conv_kernel, qk_gain, fast_init, step_size.reshape(1, 1))


def solution(mesh):
    in_specs = (
        P(None, None, ("seq", "wide"), None),
        P(),
        P(None, "wide", None),
        P(None, "wide", None, None),
        P("wide"),
    )
    out_specs = P(None, "seq", "wide")
    return jax.shard_map(local, mesh=mesh, in_specs=in_specs, out_specs=out_specs, check_vma=False)
```
